32 devices in a mesh: parts: 2 (over x), lat: 16 (over z, y, core).
Axes of the slice: x: 2, y: 2, z: 4, core: 2. Of those that a mesh axis runs over, the one named last changes fastest.
Arguments:
- grid_field: float32 [368, 1440, 256], P('lat', None, 'parts'), parts along dimension 2, may hold values from -170 to 170
- norm_gain: float32 [128], P('parts'), parts along dimension 0, may hold values from 0.5 to 1.5
- filter_weight: bfloat16 [352, 2, 64, 128], P('lat', None, None, 'parts'), parts along dimension 3, may hold values from -0.5 to 0.5
Outputs:
- spectrum_out: bfloat16 [352, 352, 512], P('lat', None, 'parts'), parts along dimension 2
The draws below stay inside these ranges and needn't reach their ends.
There are 2 independent parts, one for each index of `parts`. The reference program is written for one: setup_inputs(seed, part) draws one part's arguments, and reference() takes and returns one part's arrays. A program takes and returns all parts, laid end to end along the dimension named above; each array names one. Nothing has to cross between parts.
All inputs are finite; a program needn't handle non-finite values.
Results may differ from the reference program's by a relative error of at most 0.0064.
Values may be sent and summed in bfloat16 or wider, within the bound.
A program may use at most 192 MiB of HBM per device.

```python
import math
import jax
import jax.numpy as jnp
from jax import lax

C = 64
S = 2
NLON = 1440
DEG_DEV = 22
NLAT = 368
L = 352
M = 352
N_LAT = 16


def draw_grid_field(key, part):
    noise_key = jax.random.fold_in(key, 11)
    across_key = jax.random.fold_in(key, 12)
    offset_key = jax.random.fold_in(key, 13)
    lat_fraction = jnp.arange(NLAT, dtype=jnp.float32) / (NLAT - 1)
    noise_field = jax.random.truncated_normal(noise_key, -4.0, 4.0, (NLAT, NLON, S * C), jnp.float32)
    rise_rows = jnp.exp(lat_fraction * jnp.log(10.0))
    across = jnp.exp(jax.random.uniform(across_key, (NLON,), jnp.float32, -1.15, 1.15))
    offset = jax.random.uniform(offset_key, (S * C,), jnp.float32, -2.0, 2.0)
    return noise_field * rise_rows[:, None, None] * across[None, :, None] + offset[None, None, :]


def levels(own_key, dims, split, low, top_value):
    factor_of, own = 1.0, jax.random.fold_in(own_key, 6)
    for axis_at, shards_of in split:
        heights = jnp.exp(jax.random.uniform(jax.random.fold_in(own, axis_at), (shards_of,), jnp.float32, low / len(split), top_value / len(split)))
        factor_of = factor_of * jnp.repeat(heights, dims[axis_at] // shards_of).reshape([-1 if axis == axis_at else 1 for axis in range(len(dims))])
    return factor_of


def centred(rng, extent, deviation, reach, shards=(), kind=jnp.bfloat16):
    array = deviation * jax.random.normal(rng, extent, jnp.float32)
    if shards:
        array = array * levels(rng, extent, shards, -0.22, 0.18)
    return jnp.clip(array, -reach, reach).astype(kind)


def setup_inputs(seed: int = 0, part: int = 0) -> dict:
    splits = jax.random.split(jax.random.key(seed), 4)
    part_keys = jax.random.split(jax.random.fold_in(splits[3], part), 4)
    return {
        "grid_field": draw_grid_field(jax.random.fold_in(jax.random.fold_in(splits[3], part), 71), part),
        "norm_gain": jnp.clip(1.0 + 0.1 * jax.random.normal(part_keys[1], (C,), jnp.float32), 0.5, 1.5),
        "filter_weight": centred(part_keys[2], (L, 2, C, C), (2 * C) ** -0.5, 0.5, ((0, 16),)),
    }


def legendre_table(colatitude, orders, degrees, weight_scale):
    cosine = jnp.cos(colatitude)[:, None]
    sine_rows = jnp.sin(colatitude)
    order_sq = orders * orders
    log_start = 0.5 * jnp.log((2.0 * orders + 1.0) / (4.0 * math.pi)) + 0.5 * (lax.lgamma(orders + 0.5) - lax.lgamma(orders + 1.0) - 0.5 * math.log(math.pi))
    log_diag = log_start[None, :] + orders[None, :] * jnp.log(sine_rows)[:, None]
    start_exp = 64.0 * jnp.floor(log_diag / (64.0 * math.log(2.0)))
    start_mant = jnp.exp(log_diag - start_exp * math.log(2.0))
    weights = (weight_scale * sine_rows)[:, None]
    limit = 2.0 ** 64
    shrink = 2.0 ** (-64)

    def recurrence(state, degree):
        previous, earlier, exponent = state
        degree_value = degree.astype(orders.dtype)
        upper_coef = jnp.sqrt((4.0 * degree_value * degree_value - 1.0) / jnp.maximum(degree_value * degree_value - order_sq, 1.0))
        below = degree_value - 1.0
        lower_coef = jnp.sqrt(jnp.maximum(below * below - order_sq, 0.0) / jnp.maximum(4.0 * below * below - 1.0, 1.0))
        recurred = upper_coef * (cosine * previous - lower_coef * earlier)
        at_start = degree_value == orders
        current = jnp.where(at_start, start_mant, jnp.where(degree_value > orders, recurred, 0.0))
        exponent = jnp.where(at_start, start_exp, exponent)
        value = (weights * (current * jnp.exp2(exponent))).astype(jnp.bfloat16)
        large = jnp.abs(current) > limit
        current = jnp.where(large, current * shrink, current)
        kept = jnp.where(large, previous * shrink, previous)
        exponent = jnp.where(large, exponent + 64.0, exponent)
        return ((current, kept, exponent), value)
    zero_state = jnp.zeros((colatitude.shape[0], orders.shape[0]), colatitude.dtype)
    last_state, stacked = lax.scan(recurrence, (zero_state, zero_state, zero_state), jnp.arange(degrees, dtype=jnp.int32), unroll=8)
    return stacked

def expand_filter(filter_weight):
    real_part = filter_weight[:, 0]
    imag_part = filter_weight[:, 1]
    from_real = jnp.stack([real_part, imag_part], axis=2)
    from_imag = jnp.stack([-imag_part, real_part], axis=2)
    return jnp.stack([from_real, from_imag], axis=1)

def apply_filter(coefficients, expanded):
    shaped = coefficients.reshape(coefficients.shape[0], coefficients.shape[1], 2, S, C)
    mixed = jnp.einsum('lmrsc,lrcqo->lmqso', shaped.astype(jnp.float32), expanded.astype(jnp.float32))
    return mixed.astype(jnp.bfloat16).reshape(coefficients.shape[0], coefficients.shape[1], 2 * S * C)

def reference(grid_field, norm_gain, filter_weight):
    lat_rows = jnp.arange(NLAT, dtype=jnp.int32)
    colatitude = math.pi * (lat_rows.astype(grid_field.dtype) + 0.5) / NLAT
    sine_rows = jnp.sin(colatitude)
    denominator = NLON * jnp.sum(sine_rows)
    first_moment = jnp.einsum('j,jnx->x', sine_rows, grid_field, precision=lax.Precision.HIGHEST)
    second_moment = jnp.einsum('j,jnx->x', sine_rows, grid_field * grid_field, precision=lax.Precision.HIGHEST)
    average = first_moment / denominator
    second_moment = second_moment / denominator
    spread = jnp.sqrt(second_moment - average * average + 1e-05)
    factor = jnp.tile(norm_gain, S) / spread
    transformed = jnp.fft.rfft(grid_field, axis=1)[:, :M, :]
    raw_spectrum = jnp.stack([jnp.real(transformed), jnp.imag(transformed)], axis=2)
    raw_spectrum = raw_spectrum.at[:, 0, 0, :].add(-NLON * average)
    fourier = (raw_spectrum * factor).astype(jnp.bfloat16).reshape(NLAT, M, 2 * S * C)
    expanded = expand_filter(filter_weight)
    weight_scale = math.pi ** 1.5 / math.sqrt(NLAT * NLON)

    def order_block(block_index):
        orders = (block_index * DEG_DEV + jnp.arange(DEG_DEV, dtype=jnp.int32)).astype(colatitude.dtype)
        legendre = legendre_table(colatitude, orders, L, weight_scale)
        panel_piece = lax.dynamic_slice_in_dim(fourier, block_index * DEG_DEV, DEG_DEV, 1)
        coefficients = jnp.einsum('ljm,jmx->lmx', legendre.astype(jnp.float32), panel_piece.astype(jnp.float32)).astype(jnp.bfloat16)
        return apply_filter(coefficients, expanded)
    blocks_out = lax.map(order_block, jnp.arange(N_LAT, dtype=jnp.int32))
    return jnp.transpose(blocks_out, (1, 0, 2, 3)).reshape(L, M, 2 * S * C)
```

```python
import math

import jax
import jax.numpy as jnp
import numpy as np
from jax import lax
from jax.experimental import pallas as pl
from jax.experimental.pallas import tpu as pltpu
from jax.sharding import PartitionSpec as P

C = 64
S = 2
DEG_DEV = 22
ORDER_PAD = 24
BLOCK = 16
LANES = 128


def round_up(value, step):
    return -(-value // step) * step


def legendre_kernel(
    orders_ref, cosine_ref, weights_ref, mant_ref, exp_ref, out_ref, prev_ref, early_ref, grow_ref, rows_ref
):
    block = pl.program_id(0)
    width = cosine_ref.shape[1]
    kept_width = out_ref.shape[2]

    @pl.when(block == 0)
    def _():
        prev_ref[...] = jnp.zeros_like(prev_ref)
        early_ref[...] = jnp.zeros_like(early_ref)
        grow_ref[...] = jnp.zeros_like(grow_ref)

    orders = orders_ref[...]
    narrow = orders[:, :LANES]
    order_sq = narrow * narrow
    cosine = cosine_ref[...]
    weights = weights_ref[...]
    limit = 2.0**64
    shrink = 2.0 ** (-64)
    previous, earlier, exponent = prev_ref[...], early_ref[...], grow_ref[...]
    first = (block * BLOCK).astype(jnp.float32)

    def widen(value):
        return jnp.concatenate([value] * (width // LANES), axis=1)

    for step in range(BLOCK):
        degree = first + float(step)
        upper = jnp.sqrt(
            (4.0 * degree * degree - 1.0) / jnp.maximum(degree * degree - order_sq, 1.0)
        )
        below = degree - 1.0
        lower = jnp.sqrt(
            jnp.maximum(below * below - order_sq, 0.0)
            / jnp.maximum(jnp.full_like(order_sq, 4.0 * below * below - 1.0), 1.0)
        )
        recurred = widen(upper) * (cosine * previous - widen(lower) * earlier)
        at_start = orders == degree
        current = jnp.where(at_start, mant_ref[...], jnp.where(orders < degree, recurred, 0.0))
        exponent = jnp.where(at_start, exp_ref[...], exponent)
        value = weights * (current * jnp.exp2(exponent))
        for lane in range(width // LANES):
            rows_ref[lane, step * ORDER_PAD : (step + 1) * ORDER_PAD, :] = value[
                :, lane * LANES : (lane + 1) * LANES
            ]
        large = jnp.abs(current) > limit
        earlier = jnp.where(large, previous * shrink, previous)
        previous = jnp.where(large, current * shrink, current)
        exponent = jnp.where(large, exponent + 64.0, exponent)

    prev_ref[...] = previous
    early_ref[...] = earlier
    grow_ref[...] = exponent
    for order in range(DEG_DEV):
        for lane in range(0, width, LANES):
            cut = min(LANES, kept_width - lane)
            piece = rows_ref[lane // LANES, pl.ds(order, BLOCK, stride=ORDER_PAD), :]
            out_ref[order, :, lane : lane + cut] = piece[:, :cut].astype(out_ref.dtype)


def legendre_table(colatitude, first_order, degrees, weight_scale):
    rows = colatitude.shape[0]
    width = round_up(rows, LANES)
    colat = jnp.concatenate([colatitude, jnp.full((width - rows,), 0.5 * math.pi, jnp.float32)])
    orders = (first_order + jnp.arange(ORDER_PAD, dtype=jnp.int32)).astype(jnp.float32)
    sine_rows = jnp.sin(colat)
    log_start = 0.5 * jnp.log((2.0 * orders + 1.0) / (4.0 * math.pi)) + 0.5 * (
        lax.lgamma(orders + 0.5) - lax.lgamma(orders + 1.0) - 0.5 * math.log(math.pi)
    )
    log_diag = log_start[:, None] + orders[:, None] * jnp.log(sine_rows)[None, :]
    start_exp = 64.0 * jnp.floor(log_diag / (64.0 * math.log(2.0)))
    start_mant = jnp.exp(log_diag - start_exp * math.log(2.0))
    state = (ORDER_PAD, width)
    whole = pl.BlockSpec(state, lambda i: (0, 0))
    line = pl.BlockSpec((1, width), lambda i: (0, 0))
    return pl.pallas_call(
        legendre_kernel,
        grid=(degrees // BLOCK,),
        out_shape=jax.ShapeDtypeStruct((DEG_DEV, degrees, rows), jnp.bfloat16),
        in_specs=[whole, line, line, whole, whole],
        out_specs=pl.BlockSpec((DEG_DEV, BLOCK, rows), lambda i: (0, i, 0)),
        scratch_shapes=[
            pltpu.VMEM(state, jnp.float32),
            pltpu.VMEM(state, jnp.float32),
            pltpu.VMEM(state, jnp.float32),
            pltpu.VMEM((width // LANES, BLOCK * ORDER_PAD, LANES), jnp.float32),
        ],
        cost_estimate=pl.CostEstimate(
            flops=degrees * ORDER_PAD * width * 2000,
            bytes_accessed=DEG_DEV * degrees * rows * 2,
            transcendentals=degrees * ORDER_PAD * width,
        ),
        compiler_params=pltpu.CompilerParams(vmem_limit_bytes=24 * 1024 * 1024),
    )(
        jnp.broadcast_to(orders[:, None], state),
        jnp.cos(colat)[None, :],
        (weight_scale * sine_rows)[None, :],
        start_mant,
        start_exp,
    )


def expand_filter(filter_weight):
    real_part = filter_weight[:, 0]
    imag_part = filter_weight[:, 1]
    from_real = jnp.stack([real_part, imag_part], axis=1)
    from_imag = jnp.stack([-imag_part, real_part], axis=1)
    mixing = jnp.stack([from_real, from_imag], axis=1)
    same = jnp.eye(S, dtype=filter_weight.dtype)
    full = mixing.transpose(0, 1, 3, 2, 4)[:, :, None, :, :, None, :] * same[None, None, :, None, None, :, None]
    return full.reshape(filter_weight.shape[0], 2 * S * C, 2 * S * C)


def fourier_matrix(orders, longitudes):
    phases = (np.arange(orders)[:, None] * np.arange(longitudes)[None, :]) % longitudes
    angles = 2.0 * np.pi * phases / longitudes
    return np.stack([np.cos(angles), -np.sin(angles)]).astype(np.float32)


def body(grid_field, norm_gain, filter_weight):
    device_index = lax.axis_index("lat")
    lat_count = lax.axis_size("lat")
    band_rows, longitudes, columns = grid_field.shape
    total_lat = band_rows * lat_count
    order_count = DEG_DEV * lat_count
    all_rows = jnp.arange(total_lat, dtype=jnp.int32)
    colat_all = math.pi * (all_rows.astype(jnp.float32) + 0.5) / total_lat
    sine_all = jnp.sin(colat_all)
    own_rows = device_index * band_rows + jnp.arange(band_rows, dtype=jnp.int32)
    sine_own = jnp.sin(math.pi * (own_rows.astype(jnp.float32) + 0.5) / total_lat)

    first = jnp.einsum("j,jnx->x", sine_own, grid_field, precision=lax.Precision.HIGHEST)
    second = jnp.einsum(
        "j,jnx->x", sine_own, grid_field * grid_field, precision=lax.Precision.HIGHEST
    )
    band_mean = first / (longitudes * jnp.sum(sine_own))
    gathered = lax.all_gather(jnp.stack([first, second, band_mean]), "lat")
    denominator = longitudes * jnp.sum(sine_all)
    average = jnp.sum(gathered[:, 0], axis=0) / denominator
    mean_square = jnp.sum(gathered[:, 1], axis=0) / denominator
    spread = jnp.sqrt(mean_square - average * average + 1e-05)
    factor = jnp.tile(norm_gain, S) / spread

    table = jnp.asarray(fourier_matrix(order_count, longitudes))
    raw = jnp.einsum("rmn,jnx->rmjx", table, grid_field, precision=lax.Precision.HIGH)
    constant = (jnp.arange(2)[:, None] + jnp.arange(order_count)[None, :]) == 0
    shift = jnp.where(constant[:, :, None, None], longitudes * band_mean, 0.0)
    fourier = (raw - shift).astype(jnp.bfloat16)
    received = lax.all_to_all(fourier, "lat", split_axis=1, concat_axis=2, tiled=True)

    weight_scale = math.pi**1.5 / math.sqrt(total_lat * longitudes)
    legendre = legendre_table(colat_all, device_index * DEG_DEV, order_count, weight_scale)
    sums = jnp.einsum("mlj,rmjx->mlrx", legendre, received, preferred_element_type=jnp.float32)
    band_sums = jnp.sum(
        legendre[0].astype(jnp.float32).reshape(order_count, lat_count, band_rows), axis=2
    )
    level = jnp.dot(
        band_sums,
        longitudes * (gathered[:, 2] - average),
        precision=lax.Precision.HIGHEST,
    )
    here = (device_index == 0) & (jnp.arange(DEG_DEV)[:, None] + jnp.arange(2)[None, :] == 0)
    sums = (sums + jnp.where(here[:, None, :, None], level[None, :, None, :], 0.0)) * factor
    coefficients = lax.all_to_all(
        sums.astype(jnp.bfloat16).reshape(DEG_DEV, order_count, 2 * columns),
        "lat",
        split_axis=1,
        concat_axis=0,
        tiled=True,
    )
    mixed = jnp.einsum(
        "mlx,lxy->lmy",
        coefficients,
        expand_filter(filter_weight),
        preferred_element_type=jnp.float32,
    )
    return mixed.astype(jnp.bfloat16)


def solution(mesh):
    in_specs = (P("lat", None, "parts"), P("parts"), P("lat", None, None, "parts"))
    out_specs = P("lat", None, "parts")
    return jax.shard_map(body, mesh=mesh, in_specs=in_specs, out_specs=out_specs, check_vma=False)
```

```python
import math

import jax
import jax.numpy as jnp
import numpy as np
from jax import lax
from jax.experimental import pallas as pl
from jax.experimental.pallas import tpu as pltpu
from jax.sharding import PartitionSpec as P

C = 64
S = 2
DEG_DEV = 22
ORDER_PAD = 24
BLOCK = 16
LANES = 128


def round_up(value, step):
    return -(-value // step) * step


def legendre_kernel(
    orders_ref, cosine_ref, weights_ref, mant_ref, exp_ref, out_ref, prev_ref, early_ref, grow_ref, rows_ref
):
    block = pl.program_id(0)
    width = cosine_ref.shape[1]
    kept_width = out_ref.shape[2]

    @pl.when(block == 0)
    def _():
        prev_ref[...] = jnp.zeros_like(prev_ref)
        early_ref[...] = jnp.zeros_like(early_ref)
        grow_ref[...] = jnp.zeros_like(grow_ref)

    orders = orders_ref[...]
    narrow = orders[:, :LANES]
    order_sq = narrow * narrow
    cosine = cosine_ref[...]
    weights = weights_ref[...]
    limit = 2.0**64
    shrink = 2.0 ** (-64)
    previous, earlier, exponent = prev_ref[...], early_ref[...], grow_ref[...]
    first = (block * BLOCK).astype(jnp.float32)

    def widen(value):
        return jnp.concatenate([value] * (width // LANES), axis=1)

    for step in range(BLOCK):
        degree = first + float(step)
        upper = jnp.sqrt(
            (4.0 * degree * degree - 1.0) / jnp.maximum(degree * degree - order_sq, 1.0)
        )
        below = degree - 1.0
        lower = jnp.sqrt(
            jnp.maximum(below * below - order_sq, 0.0)
            / jnp.maximum(jnp.full_like(order_sq, 4.0 * below * below - 1.0), 1.0)
        )
        recurred = widen(upper) * (cosine * previous - widen(lower) * earlier)
        at_start = orders == degree
        current = jnp.where(at_start, mant_ref[...], jnp.where(orders < degree, recurred, 0.0))
        exponent = jnp.where(at_start, exp_ref[...], exponent)
        value = weights * (current * jnp.exp2(exponent))
        for lane in range(width // LANES):
            rows_ref[lane, step * ORDER_PAD : (step + 1) * ORDER_PAD, :] = value[
                :, lane * LANES : (lane + 1) * LANES
            ]
        large = jnp.abs(current) > limit
        earlier = jnp.where(large, previous * shrink, previous)
        previous = jnp.where(large, current * shrink, current)
        exponent = jnp.where(large, exponent + 64.0, exponent)

    prev_ref[...] = previous
    early_ref[...] = earlier
    grow_ref[...] = exponent
    for order in range(DEG_DEV):
        for lane in range(0, width, LANES):
            cut = min(LANES, kept_width - lane)
            piece = rows_ref[lane // LANES, pl.ds(order, BLOCK, stride=ORDER_PAD), :]
            out_ref[order, :, lane : lane + cut] = piece[:, :cut].astype(out_ref.dtype)


def legendre_table(colatitude, first_order, degrees, weight_scale):
    rows = colatitude.shape[0]
    width = round_up(rows, LANES)
    colat = jnp.concatenate([colatitude, jnp.full((width - rows,), 0.5 * math.pi, jnp.float32)])
    orders = (first_order + jnp.arange(ORDER_PAD, dtype=jnp.int32)).astype(jnp.float32)
    sine_rows = jnp.sin(colat)
    log_start = 0.5 * jnp.log((2.0 * orders + 1.0) / (4.0 * math.pi)) + 0.5 * (
        lax.lgamma(orders + 0.5) - lax.lgamma(orders + 1.0) - 0.5 * math.log(math.pi)
    )
    log_diag = log_start[:, None] + orders[:, None] * jnp.log(sine_rows)[None, :]
    start_exp = 64.0 * jnp.floor(log_diag / (64.0 * math.log(2.0)))
    start_mant = jnp.exp(log_diag - start_exp * math.log(2.0))
    state = (ORDER_PAD, width)
    whole = pl.BlockSpec(state, lambda i: (0, 0))
    line = pl.BlockSpec((1, width), lambda i: (0, 0))
    return pl.pallas_call(
        legendre_kernel,
        grid=(degrees // BLOCK,),
        out_shape=jax.ShapeDtypeStruct((DEG_DEV, degrees, rows), jnp.bfloat16),
        in_specs=[whole, line, line, whole, whole],
        out_specs=pl.BlockSpec((DEG_DEV, BLOCK, rows), lambda i: (0, i, 0)),
        scratch_shapes=[
            pltpu.VMEM(state, jnp.float32),
            pltpu.VMEM(state, jnp.float32),
            pltpu.VMEM(state, jnp.float32),
            pltpu.VMEM((width // LANES, BLOCK * ORDER_PAD, LANES), jnp.float32),
        ],
        cost_estimate=pl.CostEstimate(
            flops=degrees * ORDER_PAD * width * 2000,
            bytes_accessed=DEG_DEV * degrees * rows * 2,
            transcendentals=degrees * ORDER_PAD * width,
        ),
        compiler_params=pltpu.CompilerParams(vmem_limit_bytes=24 * 1024 * 1024),
    )(
        jnp.broadcast_to(orders[:, None], state),
        jnp.cos(colat)[None, :],
        (weight_scale * sine_rows)[None, :],
        start_mant,
        start_exp,
    )


def expand_filter(filter_weight):
    real_part = filter_weight[:, 0]
    imag_part = filter_weight[:, 1]
    from_real = jnp.stack([real_part, imag_part], axis=1)
    from_imag = jnp.stack([-imag_part, real_part], axis=1)
    mixing = jnp.stack([from_real, from_imag], axis=1)
    same = jnp.eye(S, dtype=filter_weight.dtype)
    full = mixing.transpose(0, 1, 3, 2, 4)[:, :, None, :, :, None, :] * same[None, None, :, None, None, :, None]
    return full.reshape(filter_weight.shape[0], 2 * S * C, 2 * S * C)


def fourier_matrix(orders, longitudes):
    phases = (np.arange(orders)[:, None] * np.arange(longitudes)[None, :]) % longitudes
    angles = 2.0 * np.pi * phases / longitudes
    return np.stack([np.cos(angles), -np.sin(angles)]).astype(np.float32)


def body(grid_field, norm_gain, filter_weight):
    device_index = lax.axis_index("lat")
    lat_count = lax.axis_size("lat")
    band_rows, longitudes, columns = grid_field.shape
    total_lat = band_rows * lat_count
    order_count = DEG_DEV * lat_count
    all_rows = jnp.arange(total_lat, dtype=jnp.int32)
    colat_all = math.pi * (all_rows.astype(jnp.float32) + 0.5) / total_lat
    sine_all = jnp.sin(colat_all)
    own_rows = device_index * band_rows + jnp.arange(band_rows, dtype=jnp.int32)
    sine_own = jnp.sin(math.pi * (own_rows.astype(jnp.float32) + 0.5) / total_lat)

    first = jnp.einsum("j,jnx->x", sine_own, grid_field, precision=lax.Precision.HIGHEST)
    second = jnp.einsum(
        "j,jnx->x", sine_own, grid_field * grid_field, precision=lax.Precision.HIGHEST
    )
    band_mean = first / (longitudes * jnp.sum(sine_own))
    gathered = lax.all_gather(jnp.stack([first, second, band_mean]), "lat")
    denominator = longitudes * jnp.sum(sine_all)
    average = jnp.sum(gathered[:, 0], axis=0) / denominator
    mean_square = jnp.sum(gathered[:, 1], axis=0) / denominator
    spread = jnp.sqrt(mean_square - average * average + 1e-05)
    factor = jnp.tile(norm_gain, S) / spread

    denominator_rows = jnp.float32(longitudes)
    cos_table, sin_table = fourier_matrix(order_count, longitudes)

    def transform(table):
        return jnp.einsum(
            "mn,jnx->mjx", jnp.asarray(table), grid_field, precision=lax.Precision.HIGH
        )

    def to_orders(raw):
        return lax.all_to_all(
            raw.astype(jnp.bfloat16), "lat", split_axis=0, concat_axis=1, tiled=True
        )

    def to_degrees(sums):
        return lax.all_to_all(
            sums.astype(jnp.bfloat16), "lat", split_axis=1, concat_axis=0, tiled=True
        )

    received_sin = to_orders(transform(sin_table))
    constant = jnp.arange(order_count) == 0
    shift = jnp.where(constant[:, None, None], denominator_rows * band_mean, 0.0)
    received_cos = to_orders(transform(cos_table) - shift)

    weight_scale = math.pi**1.5 / math.sqrt(total_lat * longitudes)
    legendre = legendre_table(colat_all, device_index * DEG_DEV, order_count, weight_scale)

    def analyse(received):
        return jnp.einsum("mlj,mjx->mlx", legendre, received, preferred_element_type=jnp.float32)

    coef_sin = to_degrees(analyse(received_sin) * factor)
    band_sums = jnp.sum(
        legendre[0].astype(jnp.float32).reshape(order_count, lat_count, band_rows), axis=2
    )
    level = jnp.dot(
        band_sums,
        denominator_rows * (gathered[:, 2] - average),
        precision=lax.Precision.HIGHEST,
    )
    here = (device_index == 0) & (jnp.arange(DEG_DEV) == 0)
    coef_cos = to_degrees(
        (analyse(received_cos) + jnp.where(here[:, None, None], level[None], 0.0)) * factor
    )

    expanded = expand_filter(filter_weight)

    def mix(coefficients, weights):
        return jnp.einsum("mlx,lxy->lmy", coefficients, weights, preferred_element_type=jnp.float32)

    mixed = mix(coef_sin, expanded[:, columns:]) + mix(coef_cos, expanded[:, :columns])
    return mixed.astype(jnp.bfloat16)


def solution(mesh):
    in_specs = (P("lat", None, "parts"), P("parts"), P("lat", None, None, "parts"))
    out_specs = P("lat", None, "parts")
    return jax.shard_map(body, mesh=mesh, in_specs=in_specs, out_specs=out_specs, check_vma=False)
```

```python
import math

import jax
import jax.numpy as jnp
import numpy as np
from jax import lax
from jax.experimental import pallas as pl
from jax.experimental.pallas import tpu as pltpu
from jax.sharding import PartitionSpec as P

C = 64
S = 2
DEG_DEV = 22
ORDER_PAD = 24
BLOCK = 16
LANES = 128


def round_up(value, step):
    return -(-value // step) * step


def legendre_kernel(
    orders_ref, cosine_ref, weights_ref, mant_ref, exp_ref, out_ref, prev_ref, early_ref, grow_ref, rows_ref
):
    block = pl.program_id(0)
    width = cosine_ref.shape[1]
    kept_width = out_ref.shape[2]

    @pl.when(block == 0)
    def _():
        prev_ref[...] = jnp.zeros_like(prev_ref)
        early_ref[...] = jnp.zeros_like(early_ref)
        grow_ref[...] = jnp.zeros_like(grow_ref)

    orders = orders_ref[...]
    narrow = orders[:, :LANES]
    order_sq = narrow * narrow
    cosine = cosine_ref[...]
    weights = weights_ref[...]
    limit = 2.0**64
    shrink = 2.0 ** (-64)
    previous, earlier, exponent = prev_ref[...], early_ref[...], grow_ref[...]
    first = (block * BLOCK).astype(jnp.float32)

    def widen(value):
        return jnp.concatenate([value] * (width // LANES), axis=1)

    for step in range(BLOCK):
        degree = first + float(step)
        upper = jnp.sqrt(
            (4.0 * degree * degree - 1.0) / jnp.maximum(degree * degree - order_sq, 1.0)
        )
        below = degree - 1.0
        lower = jnp.sqrt(
            jnp.maximum(below * below - order_sq, 0.0)
            / jnp.maximum(jnp.full_like(order_sq, 4.0 * below * below - 1.0), 1.0)
        )
        recurred = widen(upper) * (cosine * previous - widen(lower) * earlier)
        at_start = orders == degree
        current = jnp.where(at_start, mant_ref[...], jnp.where(orders < degree, recurred, 0.0))
        exponent = jnp.where(at_start, exp_ref[...], exponent)
        value = weights * (current * jnp.exp2(exponent))
        for lane in range(width // LANES):
            rows_ref[lane, step * ORDER_PAD : (step + 1) * ORDER_PAD, :] = value[
                :, lane * LANES : (lane + 1) * LANES
            ]
        large = jnp.abs(current) > limit
        earlier = jnp.where(large, previous * shrink, previous)
        previous = jnp.where(large, current * shrink, current)
        exponent = jnp.where(large, exponent + 64.0, exponent)

    prev_ref[...] = previous
    early_ref[...] = earlier
    grow_ref[...] = exponent
    for order in range(DEG_DEV):
        for lane in range(0, width, LANES):
            cut = min(LANES, kept_width - lane)
            piece = rows_ref[lane // LANES, pl.ds(order, BLOCK, stride=ORDER_PAD), :]
            out_ref[order, :, lane : lane + cut] = piece[:, :cut].astype(out_ref.dtype)


def legendre_table(colatitude, first_order, degrees, weight_scale):
    rows = colatitude.shape[0]
    width = round_up(rows, LANES)
    colat = jnp.concatenate([colatitude, jnp.full((width - rows,), 0.5 * math.pi, jnp.float32)])
    orders = (first_order + jnp.arange(ORDER_PAD, dtype=jnp.int32)).astype(jnp.float32)
    sine_rows = jnp.sin(colat)
    log_start = 0.5 * jnp.log((2.0 * orders + 1.0) / (4.0 * math.pi)) + 0.5 * (
        lax.lgamma(orders + 0.5) - lax.lgamma(orders + 1.0) - 0.5 * math.log(math.pi)
    )
    log_diag = log_start[:, None] + orders[:, None] * jnp.log(sine_rows)[None, :]
    start_exp = 64.0 * jnp.floor(log_diag / (64.0 * math.log(2.0)))
    start_mant = jnp.exp(log_diag - start_exp * math.log(2.0))
    state = (ORDER_PAD, width)
    whole = pl.BlockSpec(state, lambda i: (0, 0))
    line = pl.BlockSpec((1, width), lambda i: (0, 0))
    return pl.pallas_call(
        legendre_kernel,
        grid=(degrees // BLOCK,),
        out_shape=jax.ShapeDtypeStruct((DEG_DEV, degrees, rows), jnp.bfloat16),
        in_specs=[whole, line, line, whole, whole],
        out_specs=pl.BlockSpec((DEG_DEV, BLOCK, rows), lambda i: (0, i, 0)),
        scratch_shapes=[
            pltpu.VMEM(state, jnp.float32),
            pltpu.VMEM(state, jnp.float32),
            pltpu.VMEM(state, jnp.float32),
            pltpu.VMEM((width // LANES, BLOCK * ORDER_PAD, LANES), jnp.float32),
        ],
        cost_estimate=pl.CostEstimate(
            flops=degrees * ORDER_PAD * width * 2000,
            bytes_accessed=DEG_DEV * degrees * rows * 2,
            transcendentals=degrees * ORDER_PAD * width,
        ),
        compiler_params=pltpu.CompilerParams(vmem_limit_bytes=24 * 1024 * 1024),
    )(
        jnp.broadcast_to(orders[:, None], state),
        jnp.cos(colat)[None, :],
        (weight_scale * sine_rows)[None, :],
        start_mant,
        start_exp,
    )


def expand_filter(filter_weight):
    real_part = filter_weight[:, 0]
    imag_part = filter_weight[:, 1]
    from_real = jnp.stack([real_part, imag_part], axis=1)
    from_imag = jnp.stack([-imag_part, real_part], axis=1)
    mixing = jnp.stack([from_real, from_imag], axis=1)
    same = jnp.eye(S, dtype=filter_weight.dtype)
    full = mixing.transpose(0, 1, 3, 2, 4)[:, :, None, :, :, None, :] * same[None, None, :, None, None, :, None]
    return full.reshape(filter_weight.shape[0], 2 * S * C, 2 * S * C)


def fourier_matrix(orders, longitudes):
    phases = (np.arange(orders)[:, None] * np.arange(longitudes)[None, :]) % longitudes
    angles = 2.0 * np.pi * phases / longitudes
    return np.stack([np.cos(angles), -np.sin(angles)]).astype(np.float32)


def body(grid_field, norm_gain, filter_weight):
    device_index = lax.axis_index("lat")
    lat_count = lax.axis_size("lat")
    band_rows, longitudes, columns = grid_field.shape
    total_lat = band_rows * lat_count
    order_count = DEG_DEV * lat_count
    all_rows = jnp.arange(total_lat, dtype=jnp.int32)
    colat_all = math.pi * (all_rows.astype(jnp.float32) + 0.5) / total_lat
    sine_all = jnp.sin(colat_all)
    own_rows = device_index * band_rows + jnp.arange(band_rows, dtype=jnp.int32)
    sine_own = jnp.sin(math.pi * (own_rows.astype(jnp.float32) + 0.5) / total_lat)

    first = jnp.einsum("j,jnx->x", sine_own, grid_field, precision=lax.Precision.HIGHEST)
    second = jnp.einsum(
        "j,jnx->x", sine_own, grid_field * grid_field, precision=lax.Precision.HIGHEST
    )
    band_mean = first / (longitudes * jnp.sum(sine_own))
    denominator_rows = jnp.float32(longitudes)
    cos_table, sin_table = fourier_matrix(order_count, longitudes)

    def transform(table):
        return jnp.einsum(
            "mn,jnx->mjx", jnp.asarray(table), grid_field, precision=lax.Precision.HIGH
        )

    def to_orders(raw):
        return lax.all_to_all(
            raw.astype(jnp.bfloat16), "lat", split_axis=0, concat_axis=1, tiled=True
        )

    def to_degrees(sums):
        return lax.all_to_all(
            sums.astype(jnp.bfloat16), "lat", split_axis=1, concat_axis=0, tiled=True
        )

    received_sin = to_orders(transform(sin_table))
    constant = jnp.arange(order_count) == 0
    shift = jnp.where(constant[:, None, None], denominator_rows * band_mean, 0.0)
    received_cos = to_orders(transform(cos_table) - shift)

    weight_scale = math.pi**1.5 / math.sqrt(total_lat * longitudes)
    legendre = legendre_table(colat_all, device_index * DEG_DEV, order_count, weight_scale)

    def analyse(received):
        return jnp.einsum("mlj,mjx->mlx", legendre, received, preferred_element_type=jnp.float32)

    sums_sin = analyse(received_sin).astype(jnp.bfloat16)
    moments, sums_sin = lax.optimization_barrier(
        (jnp.stack([first, second, band_mean]), sums_sin)
    )
    gathered, sums_sin = lax.optimization_barrier((lax.all_gather(moments, "lat"), sums_sin))
    denominator = longitudes * jnp.sum(sine_all)
    average = jnp.sum(gathered[:, 0], axis=0) / denominator
    mean_square = jnp.sum(gathered[:, 1], axis=0) / denominator
    spread = jnp.sqrt(mean_square - average * average + 1e-05)
    factor = jnp.tile(norm_gain, S) / spread
    coef_sin = to_degrees(sums_sin)
    band_sums = jnp.sum(
        legendre[0].astype(jnp.float32).reshape(order_count, lat_count, band_rows), axis=2
    )
    level = jnp.dot(
        band_sums,
        denominator_rows * (gathered[:, 2] - average),
        precision=lax.Precision.HIGHEST,
    )
    here = (device_index == 0) & (jnp.arange(DEG_DEV) == 0)
    coef_cos = to_degrees(
        analyse(received_cos) + jnp.where(here[:, None, None], level[None], 0.0)
    )

    expanded = expand_filter(filter_weight)
    expanded = (expanded * jnp.tile(factor, 2)[None, :, None]).astype(jnp.bfloat16)

    def mix(coefficients, weights):
        return jnp.einsum("mlx,lxy->lmy", coefficients, weights, preferred_element_type=jnp.float32)

    mixed = mix(coef_sin, expanded[:, columns:]) + mix(coef_cos, expanded[:, :columns])
    return mixed.astype(jnp.bfloat16)


def solution(mesh):
    in_specs = (P("lat", None, "parts"), P("parts"), P("lat", None, None, "parts"))
    out_specs = P("lat", None, "parts")
    return jax.shard_map(body, mesh=mesh, in_specs=in_specs, out_specs=out_specs, check_vma=False)
```

```python
import math

import jax
import jax.numpy as jnp
import numpy as np
from jax import lax
from jax.experimental import pallas as pl
from jax.experimental.pallas import tpu as pltpu
from jax.sharding import PartitionSpec as P

C = 64
S = 2
DEG_DEV = 22
ORDER_PAD = 24
BLOCK = 16
LANES = 128


def round_up(value, step):
    return -(-value // step) * step


def legendre_kernel(
    orders_ref, cosine_ref, weights_ref, mant_ref, exp_ref, out_ref, prev_ref, early_ref, grow_ref, rows_ref
):
    block = pl.program_id(0)
    width = cosine_ref.shape[1]
    kept_width = out_ref.shape[2]

    @pl.when(block == 0)
    def _():
        prev_ref[...] = jnp.zeros_like(prev_ref)
        early_ref[...] = jnp.zeros_like(early_ref)
        grow_ref[...] = jnp.zeros_like(grow_ref)

    orders = orders_ref[...]
    narrow = orders[:, :LANES]
    order_sq = narrow * narrow
    cosine = cosine_ref[...]
    weights = weights_ref[...]
    limit = 2.0**64
    shrink = 2.0 ** (-64)
    previous, earlier, exponent = prev_ref[...], early_ref[...], grow_ref[...]
    first = (block * BLOCK).astype(jnp.float32)

    def widen(value):
        return jnp.concatenate([value] * (width // LANES), axis=1)

    for step in range(BLOCK):
        degree = first + float(step)
        upper = jnp.sqrt(
            (4.0 * degree * degree - 1.0) / jnp.maximum(degree * degree - order_sq, 1.0)
        )
        below = degree - 1.0
        lower = jnp.sqrt(
            jnp.maximum(below * below - order_sq, 0.0)
            / jnp.maximum(jnp.full_like(order_sq, 4.0 * below * below - 1.0), 1.0)
        )
        recurred = widen(upper) * (cosine * previous - widen(lower) * earlier)
        at_start = orders == degree
        current = jnp.where(at_start, mant_ref[...], jnp.where(orders < degree, recurred, 0.0))
        exponent = jnp.where(at_start, exp_ref[...], exponent)
        value = weights * (current * jnp.exp2(exponent))
        for lane in range(width // LANES):
            rows_ref[lane, step * ORDER_PAD : (step + 1) * ORDER_PAD, :] = value[
                :, lane * LANES : (lane + 1) * LANES
            ]
        large = jnp.abs(current) > limit
        earlier = jnp.where(large, previous * shrink, previous)
        previous = jnp.where(large, current * shrink, current)
        exponent = jnp.where(large, exponent + 64.0, exponent)

    prev_ref[...] = previous
    early_ref[...] = earlier
    grow_ref[...] = exponent
    for order in range(DEG_DEV):
        for lane in range(0, width, LANES):
            cut = min(LANES, kept_width - lane)
            piece = rows_ref[lane // LANES, pl.ds(order, BLOCK, stride=ORDER_PAD), :]
            out_ref[order, :, lane : lane + cut] = piece[:, :cut].astype(out_ref.dtype)


def legendre_table(colatitude, first_order, degrees, weight_scale):
    rows = colatitude.shape[0]
    width = round_up(rows, LANES)
    colat = jnp.concatenate([colatitude, jnp.full((width - rows,), 0.5 * math.pi, jnp.float32)])
    orders = (first_order + jnp.arange(ORDER_PAD, dtype=jnp.int32)).astype(jnp.float32)
    sine_rows = jnp.sin(colat)
    log_start = 0.5 * jnp.log((2.0 * orders + 1.0) / (4.0 * math.pi)) + 0.5 * (
        lax.lgamma(orders + 0.5) - lax.lgamma(orders + 1.0) - 0.5 * math.log(math.pi)
    )
    log_diag = log_start[:, None] + orders[:, None] * jnp.log(sine_rows)[None, :]
    start_exp = 64.0 * jnp.floor(log_diag / (64.0 * math.log(2.0)))
    start_mant = jnp.exp(log_diag - start_exp * math.log(2.0))
    state = (ORDER_PAD, width)
    whole = pl.BlockSpec(state, lambda i: (0, 0))
    line = pl.BlockSpec((1, width), lambda i: (0, 0))
    return pl.pallas_call(
        legendre_kernel,
        grid=(degrees // BLOCK,),
        out_shape=jax.ShapeDtypeStruct((DEG_DEV, degrees, rows), jnp.bfloat16),
        in_specs=[whole, line, line, whole, whole],
        out_specs=pl.BlockSpec((DEG_DEV, BLOCK, rows), lambda i: (0, i, 0)),
        scratch_shapes=[
            pltpu.VMEM(state, jnp.float32),
            pltpu.VMEM(state, jnp.float32),
            pltpu.VMEM(state, jnp.float32),
            pltpu.VMEM((width // LANES, BLOCK * ORDER_PAD, LANES), jnp.float32),
        ],
        cost_estimate=pl.CostEstimate(
            flops=degrees * ORDER_PAD * width * 2000,
            bytes_accessed=DEG_DEV * degrees * rows * 2,
            transcendentals=degrees * ORDER_PAD * width,
        ),
        compiler_params=pltpu.CompilerParams(vmem_limit_bytes=24 * 1024 * 1024),
    )(
        jnp.broadcast_to(orders[:, None], state),
        jnp.cos(colat)[None, :],
        (weight_scale * sine_rows)[None, :],
        start_mant,
        start_exp,
    )


def expand_filter(filter_weight):
    real_part = filter_weight[:, 0]
    imag_part = filter_weight[:, 1]
    from_real = jnp.stack([real_part, imag_part], axis=1)
    from_imag = jnp.stack([-imag_part, real_part], axis=1)
    mixing = jnp.stack([from_real, from_imag], axis=1)
    same = jnp.eye(S, dtype=filter_weight.dtype)
    full = mixing.transpose(0, 1, 3, 2, 4)[:, :, None, :, :, None, :] * same[None, None, :, None, None, :, None]
    return full.reshape(filter_weight.shape[0], 2 * S * C, 2 * S * C)


def mix_kernel(sin_ref, cos_ref, weight_ref, out_ref, rows_ref):
    sources, degrees, orders, half = cos_ref.shape
    for degree in range(degrees):
        for source in range(sources):
            rows = slice(source * orders, (source + 1) * orders)
            rows_ref[degree, rows, :half] = cos_ref[source, degree].astype(jnp.float32)
            rows_ref[degree, rows, half:] = sin_ref[source, degree].astype(jnp.float32)
        out_ref[degree] = jnp.dot(
            rows_ref[degree].astype(jnp.bfloat16),
            weight_ref[degree],
            preferred_element_type=jnp.float32,
        ).astype(out_ref.dtype)


def mix(coef_sin, coef_cos, weights):
    sources, degrees, orders, half = coef_cos.shape
    wide = weights.shape[2]
    step = 2
    piece = pl.BlockSpec((sources, step, orders, half), lambda i: (0, i, 0, 0))
    return pl.pallas_call(
        mix_kernel,
        grid=(degrees // step,),
        out_shape=jax.ShapeDtypeStruct((degrees, sources * orders, wide), jnp.bfloat16),
        in_specs=[piece, piece, pl.BlockSpec((step, 2 * half, wide), lambda i: (i, 0, 0))],
        out_specs=pl.BlockSpec((step, sources * orders, wide), lambda i: (i, 0, 0)),
        scratch_shapes=[pltpu.VMEM((step, sources * orders, 2 * half), jnp.float32)],
        compiler_params=pltpu.CompilerParams(vmem_limit_bytes=24 * 1024 * 1024),
    )(coef_sin, coef_cos, weights)


def fourier_matrix(orders, longitudes):
    phases = (np.arange(orders)[:, None] * np.arange(longitudes)[None, :]) % longitudes
    angles = 2.0 * np.pi * phases / longitudes
    return np.stack([np.cos(angles), -np.sin(angles)]).astype(np.float32)


def body(grid_field, norm_gain, filter_weight):
    device_index = lax.axis_index("lat")
    lat_count = lax.axis_size("lat")
    band_rows, longitudes, columns = grid_field.shape
    total_lat = band_rows * lat_count
    order_count = DEG_DEV * lat_count
    all_rows = jnp.arange(total_lat, dtype=jnp.int32)
    colat_all = math.pi * (all_rows.astype(jnp.float32) + 0.5) / total_lat
    sine_all = jnp.sin(colat_all)
    own_rows = device_index * band_rows + jnp.arange(band_rows, dtype=jnp.int32)
    sine_own = jnp.sin(math.pi * (own_rows.astype(jnp.float32) + 0.5) / total_lat)

    first = jnp.einsum("j,jnx->x", sine_own, grid_field, precision=lax.Precision.HIGHEST)
    second = jnp.einsum(
        "j,jnx->x", sine_own, grid_field * grid_field, precision=lax.Precision.HIGHEST
    )
    band_mean = first / (longitudes * jnp.sum(sine_own))
    denominator_rows = jnp.float32(longitudes)
    cos_table, sin_table = fourier_matrix(order_count, longitudes)

    def transform(table):
        return jnp.einsum(
            "mn,jnx->mjx", jnp.asarray(table), grid_field, precision=lax.Precision.HIGH
        )

    def to_orders(raw):
        return lax.all_to_all(
            raw.astype(jnp.bfloat16), "lat", split_axis=0, concat_axis=1, tiled=True
        )

    def to_degrees(sums):
        split = sums.astype(jnp.bfloat16).transpose(1, 0, 2)
        return lax.all_to_all(
            split.reshape(lat_count, DEG_DEV, DEG_DEV, columns), "lat", split_axis=0, concat_axis=0
        )

    received_sin = to_orders(transform(sin_table))
    constant = jnp.arange(order_count) == 0
    shift = jnp.where(constant[:, None, None], denominator_rows * band_mean, 0.0)
    received_cos = to_orders(transform(cos_table) - shift)

    weight_scale = math.pi**1.5 / math.sqrt(total_lat * longitudes)
    legendre = legendre_table(colat_all, device_index * DEG_DEV, order_count, weight_scale)

    def analyse(received):
        return jnp.einsum("mlj,mjx->mlx", legendre, received, preferred_element_type=jnp.float32)

    sums_sin = analyse(received_sin).astype(jnp.bfloat16)
    moments, sums_sin = lax.optimization_barrier(
        (jnp.stack([first, second, band_mean]), sums_sin)
    )
    gathered, sums_sin = lax.optimization_barrier((lax.all_gather(moments, "lat"), sums_sin))
    denominator = longitudes * jnp.sum(sine_all)
    average = jnp.sum(gathered[:, 0], axis=0) / denominator
    mean_square = jnp.sum(gathered[:, 1], axis=0) / denominator
    spread = jnp.sqrt(mean_square - average * average + 1e-05)
    factor = jnp.tile(norm_gain, S) / spread
    coef_sin = to_degrees(sums_sin)
    band_sums = jnp.sum(
        legendre[0].astype(jnp.float32).reshape(order_count, lat_count, band_rows), axis=2
    )
    level = jnp.dot(
        band_sums,
        denominator_rows * (gathered[:, 2] - average),
        precision=lax.Precision.HIGHEST,
    )
    here = (device_index == 0) & (jnp.arange(DEG_DEV) == 0)
    coef_cos = to_degrees(
        analyse(received_cos) + jnp.where(here[:, None, None], level[None], 0.0)
    )

    expanded = expand_filter(filter_weight)
    expanded = (expanded * jnp.tile(factor, 2)[None, :, None]).astype(jnp.bfloat16)

    return mix(coef_sin, coef_cos, expanded)


def solution(mesh):
    in_specs = (P("lat", None, "parts"), P("parts"), P("lat", None, None, "parts"))
    out_specs = P("lat", None, "parts")
    return jax.shard_map(body, mesh=mesh, in_specs=in_specs, out_specs=out_specs, check_vma=False)
```

```python
import math

import jax
import jax.numpy as jnp
import numpy as np
from jax import lax
from jax.experimental import pallas as pl
from jax.experimental.pallas import tpu as pltpu
from jax.sharding import PartitionSpec as P

C = 64
S = 2
DEG_DEV = 22
ORDER_PAD = 24
BLOCK = 16
LANES = 128


def round_up(value, step):
    return -(-value // step) * step


def legendre_kernel(
    orders_ref, cosine_ref, weights_ref, mant_ref, exp_ref, out_ref, prev_ref, early_ref, grow_ref, rows_ref
):
    block = pl.program_id(0)
    width = cosine_ref.shape[1]
    kept_width = out_ref.shape[2]

    @pl.when(block == 0)
    def _():
        prev_ref[...] = jnp.zeros_like(prev_ref)
        early_ref[...] = jnp.zeros_like(early_ref)
        grow_ref[...] = jnp.zeros_like(grow_ref)

    orders = orders_ref[...]
    narrow = orders[:, :LANES]
    order_sq = narrow * narrow
    cosine = cosine_ref[...]
    weights = weights_ref[...]
    limit = 2.0**64
    shrink = 2.0 ** (-64)
    previous, earlier, exponent = prev_ref[...], early_ref[...], grow_ref[...]
    first = (block * BLOCK).astype(jnp.float32)

    def widen(value):
        return jnp.concatenate([value] * (width // LANES), axis=1)

    for step in range(BLOCK):
        degree = first + float(step)
        upper = jnp.sqrt(
            (4.0 * degree * degree - 1.0) / jnp.maximum(degree * degree - order_sq, 1.0)
        )
        below = degree - 1.0
        lower = jnp.sqrt(
            jnp.maximum(below * below - order_sq, 0.0)
            / jnp.maximum(jnp.full_like(order_sq, 4.0 * below * below - 1.0), 1.0)
        )
        recurred = widen(upper) * (cosine * previous - widen(lower) * earlier)
        at_start = orders == degree
        current = jnp.where(at_start, mant_ref[...], jnp.where(orders < degree, recurred, 0.0))
        exponent = jnp.where(at_start, exp_ref[...], exponent)
        value = weights * (current * jnp.exp2(exponent))
        for lane in range(width // LANES):
            rows_ref[lane, step * ORDER_PAD : (step + 1) * ORDER_PAD, :] = value[
                :, lane * LANES : (lane + 1) * LANES
            ]
        large = jnp.abs(current) > limit
        earlier = jnp.where(large, previous * shrink, previous)
        previous = jnp.where(large, current * shrink, current)
        exponent = jnp.where(large, exponent + 64.0, exponent)

    prev_ref[...] = previous
    early_ref[...] = earlier
    grow_ref[...] = exponent
    for order in range(DEG_DEV):
        for lane in range(0, width, LANES):
            cut = min(LANES, kept_width - lane)
            piece = rows_ref[lane // LANES, pl.ds(order, BLOCK, stride=ORDER_PAD), :]
            out_ref[order, :, lane : lane + cut] = piece[:, :cut].astype(out_ref.dtype)


def legendre_table(colatitude, first_order, degrees, weight_scale):
    rows = colatitude.shape[0]
    width = round_up(rows, LANES)
    colat = jnp.concatenate([colatitude, jnp.full((width - rows,), 0.5 * math.pi, jnp.float32)])
    orders = (first_order + jnp.arange(ORDER_PAD, dtype=jnp.int32)).astype(jnp.float32)
    sine_rows = jnp.sin(colat)
    log_start = 0.5 * jnp.log((2.0 * orders + 1.0) / (4.0 * math.pi)) + 0.5 * (
        lax.lgamma(orders + 0.5) - lax.lgamma(orders + 1.0) - 0.5 * math.log(math.pi)
    )
    log_diag = log_start[:, None] + orders[:, None] * jnp.log(sine_rows)[None, :]
    start_exp = 64.0 * jnp.floor(log_diag / (64.0 * math.log(2.0)))
    start_mant = jnp.exp(log_diag - start_exp * math.log(2.0))
    state = (ORDER_PAD, width)
    whole = pl.BlockSpec(state, lambda i: (0, 0))
    line = pl.BlockSpec((1, width), lambda i: (0, 0))
    return pl.pallas_call(
        legendre_kernel,
        grid=(degrees // BLOCK,),
        out_shape=jax.ShapeDtypeStruct((DEG_DEV, degrees, rows), jnp.bfloat16),
        in_specs=[whole, line, line, whole, whole],
        out_specs=pl.BlockSpec((DEG_DEV, BLOCK, rows), lambda i: (0, i, 0)),
        scratch_shapes=[
            pltpu.VMEM(state, jnp.float32),
            pltpu.VMEM(state, jnp.float32),
            pltpu.VMEM(state, jnp.float32),
            pltpu.VMEM((width // LANES, BLOCK * ORDER_PAD, LANES), jnp.float32),
        ],
        cost_estimate=pl.CostEstimate(
            flops=degrees * ORDER_PAD * width * 2000,
            bytes_accessed=DEG_DEV * degrees * rows * 2,
            transcendentals=degrees * ORDER_PAD * width,
        ),
        compiler_params=pltpu.CompilerParams(vmem_limit_bytes=24 * 1024 * 1024),
    )(
        jnp.broadcast_to(orders[:, None], state),
        jnp.cos(colat)[None, :],
        (weight_scale * sine_rows)[None, :],
        start_mant,
        start_exp,
    )


def expand_filter(filter_weight):
    real_part = filter_weight[:, 0]
    imag_part = filter_weight[:, 1]
    from_real = jnp.stack([real_part, imag_part], axis=1)
    from_imag = jnp.stack([-imag_part, real_part], axis=1)
    mixing = jnp.stack([from_real, from_imag], axis=1)
    same = jnp.eye(S, dtype=filter_weight.dtype)
    full = mixing.transpose(0, 1, 3, 2, 4)[:, :, None, :, :, None, :] * same[None, None, :, None, None, :, None]
    return full.reshape(filter_weight.shape[0], 2 * S * C, 2 * S * C)


def mix_kernel(sin_ref, cos_ref, weight_ref, out_ref, rows_ref):
    sources, degrees, orders, half = cos_ref.shape
    for degree in range(degrees):
        for source in range(sources):
            rows = slice(source * orders, (source + 1) * orders)
            rows_ref[degree, rows, :half] = cos_ref[source, degree].astype(jnp.float32)
            rows_ref[degree, rows, half:] = sin_ref[source, degree].astype(jnp.float32)
        out_ref[degree] = jnp.dot(
            rows_ref[degree].astype(jnp.bfloat16),
            weight_ref[degree],
            preferred_element_type=jnp.float32,
        ).astype(out_ref.dtype)


def mix(coef_sin, coef_cos, weights):
    sources, degrees, orders, half = coef_cos.shape
    wide = weights.shape[2]
    step = 2
    piece = pl.BlockSpec((sources, step, orders, half), lambda i: (0, i, 0, 0))
    return pl.pallas_call(
        mix_kernel,
        grid=(degrees // step,),
        out_shape=jax.ShapeDtypeStruct((degrees, sources * orders, wide), jnp.bfloat16),
        in_specs=[piece, piece, pl.BlockSpec((step, 2 * half, wide), lambda i: (i, 0, 0))],
        out_specs=pl.BlockSpec((step, sources * orders, wide), lambda i: (i, 0, 0)),
        scratch_shapes=[pltpu.VMEM((step, sources * orders, 2 * half), jnp.float32)],
        compiler_params=pltpu.CompilerParams(vmem_limit_bytes=24 * 1024 * 1024),
    )(coef_sin, coef_cos, weights)


def fourier_matrix(orders, longitudes):
    phases = (np.arange(orders)[:, None] * np.arange(longitudes)[None, :]) % longitudes
    angles = 2.0 * np.pi * phases / longitudes
    return np.stack([np.cos(angles), -np.sin(angles)]).astype(np.float32)


def body(grid_field, norm_gain, filter_weight):
    device_index = lax.axis_index("lat")
    lat_count = lax.axis_size("lat")
    band_rows, longitudes, columns = grid_field.shape
    total_lat = band_rows * lat_count
    order_count = DEG_DEV * lat_count
    all_rows = jnp.arange(total_lat, dtype=jnp.int32)
    colat_all = math.pi * (all_rows.astype(jnp.float32) + 0.5) / total_lat
    sine_all = jnp.sin(colat_all)
    own_rows = device_index * band_rows + jnp.arange(band_rows, dtype=jnp.int32)
    sine_own = jnp.sin(math.pi * (own_rows.astype(jnp.float32) + 0.5) / total_lat)

    first = jnp.einsum("j,jnx->x", sine_own, grid_field, precision=lax.Precision.HIGHEST)
    second = jnp.einsum(
        "j,jnx->x", sine_own, grid_field * grid_field, precision=lax.Precision.HIGHEST
    )
    band_mean = first / (longitudes * jnp.sum(sine_own))
    denominator_rows = jnp.float32(longitudes)
    cos_table, sin_table = fourier_matrix(order_count, longitudes)

    def transform(table):
        return jnp.einsum(
            "mn,jnx->mjx", jnp.asarray(table), grid_field, precision=lax.Precision.HIGH
        )

    def to_orders(raw):
        return lax.all_to_all(
            raw.astype(jnp.bfloat16), "lat", split_axis=0, concat_axis=1, tiled=True
        )

    def to_degrees(sums):
        return lax.all_to_all(
            sums, "lat", split_axis=0, concat_axis=0
        )

    received_sin = to_orders(transform(sin_table))
    constant = jnp.arange(order_count) == 0
    shift = jnp.where(constant[:, None, None], denominator_rows * band_mean, 0.0)
    received_cos = to_orders(transform(cos_table) - shift)

    weight_scale = math.pi**1.5 / math.sqrt(total_lat * longitudes)
    legendre = legendre_table(colat_all, device_index * DEG_DEV, order_count, weight_scale)

    def analyse(received):
        return jnp.einsum("mlj,mjx->mlx", legendre, received, preferred_element_type=jnp.float32)

    def by_degree(sums):
        ordered = sums.astype(jnp.bfloat16).transpose(1, 0, 2)
        return ordered.reshape(lat_count, DEG_DEV, DEG_DEV, columns)

    sums_sin = by_degree(analyse(received_sin))
    moments, sums_sin = lax.optimization_barrier(
        (jnp.stack([first, second, band_mean]), sums_sin)
    )
    gathered, sums_sin = lax.optimization_barrier((lax.all_gather(moments, "lat"), sums_sin))
    denominator = longitudes * jnp.sum(sine_all)
    average = jnp.sum(gathered[:, 0], axis=0) / denominator
    mean_square = jnp.sum(gathered[:, 1], axis=0) / denominator
    spread = jnp.sqrt(mean_square - average * average + 1e-05)
    factor = jnp.tile(norm_gain, S) / spread
    coef_sin = to_degrees(sums_sin)
    band_sums = jnp.sum(
        legendre[0].astype(jnp.float32).reshape(order_count, lat_count, band_rows), axis=2
    )
    level = jnp.dot(
        band_sums,
        denominator_rows * (gathered[:, 2] - average),
        precision=lax.Precision.HIGHEST,
    )
    here = (device_index == 0) & (jnp.arange(DEG_DEV) == 0)
    coef_cos = to_degrees(
        by_degree(analyse(received_cos) + jnp.where(here[:, None, None], level[None], 0.0))
    )

    expanded = expand_filter(filter_weight)
    expanded = (expanded * jnp.tile(factor, 2)[None, :, None]).astype(jnp.bfloat16)

    return mix(coef_sin, coef_cos, expanded)


def solution(mesh):
    in_specs = (P("lat", None, "parts"), P("parts"), P("lat", None, None, "parts"))
    out_specs = P("lat", None, "parts")
    return jax.shard_map(body, mesh=mesh, in_specs=in_specs, out_specs=out_specs, check_vma=False)
```
